32 devices in a mesh: row: 8 (over z, x), col: 4 (over y, core).
Axes of the slice: x: 2, y: 2, z: 4, core: 2. Of those that a mesh axis runs over, the one named last changes fastest.
Arguments:
- right_sides: bfloat16 [4, 32, 256, 256], P(None, ('row', 'col')), may hold values from -6 to 6
- lower_blocks: bfloat16 [8, 4, 3, 6, 256, 256], P('row', 'col'), may hold values from -0.1875 to 0.1875
- lower_source: int32 [8, 4, 3, 6], P('row', 'col'), may hold values from 0 to 7
- lower_target: int32 [8, 4, 3, 6], P('row', 'col'), may hold values from 4 to 16, as said below
- diag_lower_inv: bfloat16 [4, 32, 256, 256], P(None, ('row', 'col')), may hold values from -1 to 2, as said below
- upper_blocks: bfloat16 [8, 4, 3, 6, 256, 256], P('row', 'col'), may hold values from -0.1875 to 0.1875
- upper_source: int32 [8, 4, 3, 6], P('row', 'col'), may hold values from 0 to 7
- upper_target: int32 [8, 4, 3, 6], P('row', 'col'), may hold values from 0 to 16, as said below
- diag_upper_inv: bfloat16 [4, 32, 256, 256], P(None, ('row', 'col')), may hold values from -1 to 2, as said below
Outputs:
- solution: float32 [4, 32, 256, 256], P(None, ('row', 'col'))
The draws below stay inside these ranges and needn't reach their ends.
Inputs may be any that keep to these rules, and one draw needn't show every extreme that they name: lower_target[r, c, a, k] is 16 for an empty slot, else b * 4 + q with a < b < 4 and 0 <= q < 4. upper_target[r, c, a, k] is 16 for an empty slot, else b * 4 + q with 0 <= b <= a and 0 <= q < 4. `diag_lower_inv`: each block is lower triangular with a positive diagonal. `diag_upper_inv`: each block is upper triangular with a positive diagonal.
All inputs are finite; a program needn't handle non-finite values.
Results may differ from the reference program's by a relative error of at most 0.029.
Values may be sent and summed in bfloat16 or wider, within the bound.
A program may use at most 128 MiB of HBM per device.

```python
import math
import jax
import jax.numpy as jnp
from jax import lax

W = 256
RHS = 256
LEV = 4
NB = 6
SPD = 1
PROC_ROWS = 8
PROC_COLS = 4
LOCAL = 4
SOURCES = 8
SUPER = 32


def level_targets(key, is_lower):
    draw_shape = (PROC_ROWS, PROC_COLS, LEV - 1, NB)
    level_key, place_key, live_key = jax.random.split(key, 3)
    source_level = lax.broadcasted_iota(jnp.int32, draw_shape, 2)
    if is_lower:
        target_level = jax.random.randint(level_key, draw_shape, source_level + 1, LEV)
        forced = LOCAL
    else:
        target_level = jax.random.randint(level_key, draw_shape, jnp.zeros(draw_shape, jnp.int32), source_level + 1)
        forced = 0
    position = jax.random.randint(place_key, draw_shape, 0, LOCAL)
    is_live = jax.random.randint(live_key, draw_shape, 0, 5) < 3
    target = jnp.where(is_live, target_level * LOCAL + position, LEV * LOCAL).astype(jnp.int32)
    target = target.at[0, 0, 0, 0].set(forced)
    return target.at[0, 0, 0, NB - 1].set(LEV * LOCAL)


def draw_lower_target(key, part):
    return level_targets(jax.random.fold_in(key, 11), True)


def draw_upper_target(key, part):
    return level_targets(jax.random.fold_in(key, 12), False)


def triangle(key, is_lower):
    draw_shape = (LEV, SUPER, W, W)
    off_key, diag_key = jax.random.split(key)
    row_pos = lax.broadcasted_iota(jnp.int32, draw_shape, 2)
    col_pos = lax.broadcasted_iota(jnp.int32, draw_shape, 3)
    off_diag = jax.random.normal(off_key, draw_shape, jnp.float32) * (0.6 / math.sqrt(W))
    diagonal = jnp.exp(jax.random.uniform(diag_key, draw_shape, jnp.float32, math.log(0.5), math.log(2.0)))
    if is_lower:
        keep_mask = row_pos > col_pos
    else:
        keep_mask = row_pos < col_pos
    values = jnp.where(row_pos == col_pos, diagonal, jnp.where(keep_mask, off_diag, 0.0))
    return values.astype(jnp.bfloat16)


def draw_diag_lower_inv(key, part):
    return triangle(jax.random.fold_in(key, 21), True)


def draw_diag_upper_inv(key, part):
    return triangle(jax.random.fold_in(key, 22), False)


def plant(drawn, rng, low, high):
    shape = drawn.shape
    index_at = [jax.random.randint(jax.random.fold_in(rng, axis), (), 0, shape[axis]) for axis in range(len(shape))]
    drawn = drawn.at[tuple(index_at)].set(low)
    longest = shape.index(max(shape))
    index_at[longest] = (index_at[longest] + 1) % shape[longest]
    return drawn.at[tuple(index_at)].set(high)


def steps_of(rng, shape, shards, low, high):
    gain = 1.0
    for axis_at, blocks in shards:
        steps = jax.random.uniform(jax.random.fold_in(jax.random.fold_in(rng, 6), axis_at), (blocks,), jnp.float32, low / len(shards), high / len(shards))
        gain = gain * jnp.repeat(jnp.exp(steps), shape[axis_at] // blocks).reshape((-1,) + (1,) * (len(shape) - 1 - axis_at))
    return gain


def centred(rng, extent, spread, bound, shards=(), kind=jnp.bfloat16):
    loudness = steps_of(rng, extent, shards, -0.22, 0.18) if shards else 1.0
    drawn = jax.random.normal(rng, extent, jnp.float32) * spread * loudness
    return jnp.minimum(jnp.maximum(drawn, -bound), bound).astype(kind)


def setup_inputs(seed: int = 0) -> dict:
    seeds = jax.random.split(jax.random.key(seed), 10)
    return {
        "right_sides": centred(seeds[0], (LEV, SUPER, W, RHS), 1.0, 6.0, ((1, 32),)),
        "lower_blocks": centred(seeds[1], (PROC_ROWS, PROC_COLS, LEV - 1, NB, W, W), (4 * W) ** -0.5, 0.1875, ((0, 8), (1, 4))),
        "lower_source": plant(jax.random.randint(seeds[2], (PROC_ROWS, PROC_COLS, LEV - 1, NB), 0, SOURCES), jax.random.fold_in(seeds[2], 1), 0, SOURCES - 1).astype(jnp.int32),
        "lower_target": draw_lower_target(jax.random.fold_in(seeds[9], 71), 0),
        "diag_lower_inv": draw_diag_lower_inv(jax.random.fold_in(seeds[9], 71), 0),
        "upper_blocks": centred(seeds[5], (PROC_ROWS, PROC_COLS, LEV - 1, NB, W, W), (4 * W) ** -0.5, 0.1875, ((0, 8), (1, 4))),
        "upper_source": plant(jax.random.randint(seeds[6], (PROC_ROWS, PROC_COLS, LEV - 1, NB), 0, SOURCES), jax.random.fold_in(seeds[6], 1), 0, SOURCES - 1).astype(jnp.int32),
        "upper_target": draw_upper_target(jax.random.fold_in(seeds[9], 71), 0),
        "diag_upper_inv": draw_diag_upper_inv(jax.random.fold_in(seeds[9], 71), 0),
    }


def round_trip(values):
    return lax.optimization_barrier(values.astype(jnp.bfloat16)).astype(jnp.float32)


def row_totals(partial_value, tree_level):
    rounded = round_trip(partial_value[:, :, tree_level])
    row_total = jnp.sum(rounded, axis=1)
    return row_total.reshape(SUPER, W, RHS)


def solve_diag(inverse, vector):
    return jnp.einsum("sij,sjm->sim", inverse.astype(jnp.float32), vector.astype(jnp.float32), precision=lax.Precision.HIGHEST)


def add_level(partial_value, blocks, source, target, solved_panel):
    panel_grid = solved_panel.reshape(PROC_ROWS, PROC_COLS, SPD, W, RHS)
    col_indices = jnp.arange(PROC_COLS, dtype=jnp.int32)

    def one_col(col_blocks, col_source, col_target, col_index):
        chosen = panel_grid[col_source // SPD, col_index, col_source % SPD]
        products = jnp.einsum("kij,kjm->kim", col_blocks.astype(jnp.float32), chosen.astype(jnp.float32), precision=lax.Precision.HIGHEST)
        summed = jax.ops.segment_sum(products, col_target, num_segments=LEV * LOCAL + 1)
        return summed[:LEV * LOCAL]

    def one_row(row_index, accumulated):
        row_blocks = lax.dynamic_index_in_dim(blocks, row_index, 0, keepdims=False)
        row_source = lax.dynamic_index_in_dim(source, row_index, 0, keepdims=False)
        row_target = lax.dynamic_index_in_dim(target, row_index, 0, keepdims=False)
        row_terms = jax.vmap(one_col)(row_blocks, row_source, row_target, col_indices)
        row_terms = row_terms.reshape(PROC_COLS, LEV, LOCAL, W, RHS)
        current = lax.dynamic_index_in_dim(accumulated, row_index, 0, keepdims=False)
        return lax.dynamic_update_index_in_dim(accumulated, current + row_terms, row_index, 0)

    return lax.fori_loop(0, PROC_ROWS, one_row, partial_value)


def reference(right_sides, lower_blocks, lower_source, lower_target, diag_lower_inv, upper_blocks, upper_source, upper_target, diag_upper_inv):
    buffer_shape = (PROC_ROWS, PROC_COLS, LEV, LOCAL, W, RHS)
    partial_value = jnp.zeros(buffer_shape, jnp.float32)
    forward = []
    for tree_level in range(LEV):
        row_total = row_totals(partial_value, tree_level)
        lowered = (right_sides[tree_level].astype(jnp.float32) - row_total).astype(jnp.bfloat16)
        result = solve_diag(diag_lower_inv[tree_level], lowered)
        forward.append(result)
        if tree_level + 1 < LEV:
            partial_value = add_level(partial_value, lower_blocks[:, :, tree_level], lower_source[:, :, tree_level], lower_target[:, :, tree_level], result.astype(jnp.bfloat16))
    partial_value = jnp.zeros(buffer_shape, jnp.float32)
    solution = [None] * LEV
    for tree_level in range(LEV - 1, -1, -1):
        row_total = row_totals(partial_value, tree_level)
        raised = (forward[tree_level] - row_total).astype(jnp.bfloat16)
        result = solve_diag(diag_upper_inv[tree_level], raised)
        solution[tree_level] = result
        if tree_level > 0:
            partial_value = add_level(partial_value, upper_blocks[:, :, tree_level - 1], upper_source[:, :, tree_level - 1], upper_target[:, :, tree_level - 1], result.astype(jnp.bfloat16))
    return jnp.stack(solution)
```

```python
import functools

import jax
import jax.numpy as jnp
from jax import lax
from jax.experimental import pallas as pl
from jax.experimental.pallas import tpu as pltpu
from jax.sharding import PartitionSpec as P

MESH = pl.DeviceIdType.MESH
CHUNKS = 2
F32 = jnp.float32
BF16 = jnp.bfloat16


def kernel(
    rows,
    cols,
    levels,
    slots,
    width,
    lanes,
    rhs_ref,
    lower_ref,
    lower_source,
    lower_target,
    diag_lower,
    upper_ref,
    upper_source,
    upper_target,
    diag_upper,
    out_ref,
    *scratch,
):
    rounds = 2 * (levels - 1)
    panels = scratch[: rounds * CHUNKS]
    forward, far, products, owned, outbox, inbox, gather_send, gather_recv, sum_send, sum_recv = scratch[
        rounds * CHUNKS :
    ]
    major = 4 if rows % 4 == 0 else 1
    minor = rows // major
    row, col = lax.axis_index("row"), lax.axis_index("col")
    row_major, row_minor = row // minor, row % minor

    def row_at(major_step, minor_step):
        return ((row_major + major_step) % major) * minor + (row_minor + minor_step) % minor

    peers = [(row_at(step, 0), col) for step in range(1, major)]
    peers += [(row_at(0, step), col) for step in range(1, minor)]
    peers += [(row, (col + step) % cols) for step in range(1, cols)]
    barrier = pltpu.get_barrier_semaphore()
    for peer in peers:
        pl.semaphore_signal(barrier, inc=1, device_id=peer, device_id_type=MESH)

    def lanes_of(chunk):
        return slice(chunk * lanes, (chunk + 1) * lanes)

    def plan(step):
        if step < levels - 1:
            return step, step + 1, lower_ref, lower_source, lower_target, step == 0, list(range(step + 2, levels))
        source = 2 * (levels - 1) - step
        first = step == levels - 1
        return source - 1, source - 1, upper_ref, upper_source, upper_target, first, list(range(source - 1))

    def far_slot(step, level):
        return level - 2 if step < levels - 1 else level

    pending = {}

    def push(step, chunk, slot, target, index):
        ref = panels[step * CHUNKS + chunk]
        copy = pltpu.make_async_remote_copy(
            src_ref=ref.at[slot],
            dst_ref=ref.at[slot],
            send_sem=gather_send.at[chunk, index],
            recv_sem=gather_recv.at[step, chunk, slot],
            device_id=(target, col),
            device_id_type=MESH,
        )
        copy.start()
        pending.setdefault(("gather", step, chunk), []).append(copy)

    def arrived(step, chunk, slot):
        ref = panels[step * CHUNKS + chunk]
        pltpu.make_async_remote_copy(
            src_ref=ref.at[slot],
            dst_ref=ref.at[slot],
            send_sem=gather_send.at[chunk, 0],
            recv_sem=gather_recv.at[step, chunk, slot],
            device_id=(row, col),
            device_id_type=MESH,
        ).wait_recv()

    def drain(kind, step, chunk):
        for copy in pending.pop((kind, step, chunk), []):
            copy.wait_send()

    def gather_start(step, chunk):
        for offset in range(1, minor):
            push(step, chunk, row, row_at(0, offset), offset - 1)
        for offset in range(1, major):
            push(step, chunk, row, row_at(offset, 0), minor - 1 + offset - 1)

    def gather_forward(step, chunk, offset):
        slot = row_at(offset, 0)
        arrived(step, chunk, slot)
        base = (minor - 1) + (major - 1) + (offset - 1) * (minor - 1)
        for across in range(1, minor):
            push(step, chunk, slot, row_at(0, across), base + across - 1)

    def gather_finish(step, chunk):
        for across in range(1, minor):
            for offset in range(major):
                arrived(step, chunk, row_at(offset, across))

    def picked(target_ref, at, wanted):
        total = jnp.zeros((width, lanes), F32)
        for k in range(slots):
            mask = jnp.full((width, lanes), target_ref[0, 0, at, k], jnp.int32) == wanted
            total = total + jnp.where(mask, products[k], 0.0)
        return total

    def update_near(step, chunk):
        at, level, blocks, source, target, first, _ = plan(step)
        ref = panels[step * CHUNKS + chunk]
        for k in range(slots):
            products[k] = jnp.dot(blocks[0, 0, at, k], ref[source[0, 0, at, k]], preferred_element_type=F32)
        drain("sum", step - 1, chunk)
        for offset in list(range(1, cols)) + [0]:
            owner = (col + offset) % cols
            total = picked(target, at, level * cols + owner)
            if not first:
                total = total + far[far_slot(step, level), owner, chunk]
            if offset == 0:
                owned[chunk] = total.astype(BF16)
                continue
            outbox[step, chunk, offset - 1] = total.astype(BF16)
            copy = pltpu.make_async_remote_copy(
                src_ref=outbox.at[step, chunk, offset - 1],
                dst_ref=inbox.at[step, chunk, offset - 1],
                send_sem=sum_send.at[chunk, offset - 1],
                recv_sem=sum_recv.at[step, chunk, offset - 1],
                device_id=(row, owner),
                device_id_type=MESH,
            )
            copy.start()
            pending.setdefault(("sum", step, chunk), []).append(copy)

    def update_far(step, chunk):
        at, _, _, _, target, first, others = plan(step)
        for level in others:
            place = far_slot(step, level)

            @pl.loop(0, cols)
            def _(q):
                total = picked(target, at, level * cols + q)
                if not first:
                    total = total + far[place, q, chunk]
                far[place, q, chunk] = total

    def finish_sum(step, chunk):
        level = plan(step)[1]
        total = owned[chunk].astype(F32)
        for copy in pending[("sum", step, chunk)]:
            copy.wait_recv()
        for offset in range(1, cols):
            total = total + inbox[step, chunk, offset - 1].astype(F32)
        if step < levels - 1:
            solve_lower(level, chunk, rhs_ref[level, 0, :, lanes_of(chunk)].astype(F32) - total)
        else:
            solve_upper(level, chunk, forward[level, chunk] - total)

    def publish(step, chunk, result):
        if step < rounds:
            panels[step * CHUNKS + chunk][row] = result.astype(BF16)
            drain("gather", step - 1, chunk)

    def solve_lower(level, chunk, lowered):
        result = jnp.dot(diag_lower[level, 0], lowered.astype(BF16), preferred_element_type=F32)
        forward[level, chunk] = result
        if level == levels - 1:
            solve_upper(level, chunk, result)
        else:
            publish(level, chunk, result)

    def solve_upper(level, chunk, raised):
        result = jnp.dot(diag_upper[level, 0], raised.astype(BF16), preferred_element_type=F32)
        out_ref[level, 0, :, lanes_of(chunk)] = result
        publish(2 * (levels - 1) - level, chunk, result)

    for chunk in range(CHUNKS):
        solve_lower(0, chunk, rhs_ref[0, 0, :, lanes_of(chunk)].astype(F32))
    pl.semaphore_wait(barrier, len(peers))

    def turn(step, chunk, other_step):
        moving = other_step is not None and other_step < rounds
        other = 1 - chunk
        gather_finish(step, chunk)
        update_near(step, chunk)
        if moving and major > 1:
            gather_forward(other_step, other, 1)
        update_far(step, chunk)
        if moving:
            for offset in range(2, major - 1):
                gather_forward(other_step, other, offset)
        finish_sum(step, chunk)
        if step + 1 < rounds:
            gather_start(step + 1, chunk)
        if moving and major > 2:
            gather_forward(other_step, other, major - 1)

    gather_start(0, 0)
    gather_start(0, 1)
    for offset in range(1, major):
        gather_forward(0, 0, offset)
    for step in range(rounds):
        turn(step, 0, step)
        turn(step, 1, step + 1)
    for kind in ("gather", "sum"):
        for chunk in range(CHUNKS):
            drain(kind, rounds - 1, chunk)


def shards(*args):
    rows, cols = lax.axis_size("row"), lax.axis_size("col")
    levels, per_device, width, rhs_cols = args[0].shape
    slots = args[1].shape[3]
    assert per_device == 1 and rhs_cols % CHUNKS == 0 and levels > 2
    lanes = rhs_cols // CHUNKS
    rounds = 2 * (levels - 1)
    major = 4 if rows % 4 == 0 else 1
    minor = rows // major
    copies = (minor - 1) + (major - 1) + (major - 1) * (minor - 1)
    vmem = pl.BlockSpec(memory_space=pltpu.VMEM)
    smem = pl.BlockSpec(memory_space=pltpu.SMEM)
    scratch = [pltpu.VMEM((rows, width, lanes), BF16) for _ in range(rounds * CHUNKS)]
    scratch += [
        pltpu.VMEM((levels, CHUNKS, width, lanes), F32),
        pltpu.VMEM((levels - 2, cols, CHUNKS, width, lanes), F32),
        pltpu.VMEM((slots, width, lanes), F32),
        pltpu.VMEM((CHUNKS, width, lanes), BF16),
        pltpu.VMEM((rounds, CHUNKS, cols - 1, width, lanes), BF16),
        pltpu.VMEM((rounds, CHUNKS, cols - 1, width, lanes), BF16),
        pltpu.SemaphoreType.DMA((CHUNKS, copies)),
        pltpu.SemaphoreType.DMA((rounds, CHUNKS, rows)),
        pltpu.SemaphoreType.DMA((CHUNKS, cols - 1)),
        pltpu.SemaphoreType.DMA((rounds, CHUNKS, cols - 1)),
    ]
    return pl.pallas_call(
        functools.partial(kernel, rows, cols, levels, slots, width, lanes),
        out_shape=jax.ShapeDtypeStruct(args[0].shape, F32),
        in_specs=[vmem, vmem, smem, smem, vmem, vmem, smem, smem, vmem],
        out_specs=vmem,
        scratch_shapes=scratch,
        compiler_params=pltpu.CompilerParams(
            collective_id=0, has_side_effects=True, vmem_limit_bytes=60 * 1024 * 1024
        ),
    )(*args)


def solution(mesh):
    in_specs = (
        P(None, ("row", "col"), None, None),
        P("row", "col", None, None, None, None),
        P("row", "col", None, None),
        P("row", "col", None, None),
        P(None, ("row", "col"), None, None),
        P("row", "col", None, None, None, None),
        P("row", "col", None, None),
        P("row", "col", None, None),
        P(None, ("row", "col"), None, None),
    )
    out_specs = P(None, ("row", "col"), None, None)
    return jax.shard_map(shards, mesh=mesh, in_specs=in_specs, out_specs=out_specs, check_vma=False)
```

```python
import functools

import jax
import jax.numpy as jnp
from jax import lax
from jax.experimental import pallas as pl
from jax.experimental.pallas import tpu as pltpu
from jax.sharding import PartitionSpec as P

MESH = pl.DeviceIdType.MESH
CHUNKS = 2
F32 = jnp.float32
BF16 = jnp.bfloat16


def kernel(
    rows,
    cols,
    levels,
    slots,
    width,
    lanes,
    rhs_hbm,
    lower_hbm,
    lower_source,
    lower_target,
    diag_lower_hbm,
    upper_hbm,
    upper_source,
    upper_target,
    diag_upper_hbm,
    out_hbm,
    *scratch,
):
    rounds = 2 * (levels - 1)
    panels = scratch[: rounds * CHUNKS]
    rest = scratch[rounds * CHUNKS :]
    forward, far, products, owned, outbox, inbox, gather_send, gather_recv, sum_send, sum_recv = rest[:10]
    inputs, out_ref, load_sem, store_sem = rest[10:15], rest[15], rest[16], rest[17]
    sources = (rhs_hbm, diag_lower_hbm, lower_hbm.at[0, 0], diag_upper_hbm, upper_hbm.at[0, 0])
    order = [(0, 0), (1, 0), (2, 0)]
    for level in range(1, levels):
        order += [(0, level), (1, level)] + ([(2, level)] if level < levels - 1 else [])
    for level in range(levels - 1, -1, -1):
        order += [(3, level)] + ([(4, level - 1)] if level else [])
    loaded = set()

    def fetch(ref, index):
        return pltpu.make_async_copy(sources[ref].at[index], inputs[ref].at[index], load_sem.at[ref, index])

    def load(ref, index):
        if (ref, index) not in loaded:
            loaded.add((ref, index))
            fetch(ref, index).wait()
        return inputs[ref].at[index]

    def store(level):
        return pltpu.make_async_copy(out_ref.at[level], out_hbm.at[level], store_sem.at[level])

    major = 4 if rows % 4 == 0 else 1
    minor = rows // major
    row, col = lax.axis_index("row"), lax.axis_index("col")
    row_major, row_minor = row // minor, row % minor

    def row_at(major_step, minor_step):
        return ((row_major + major_step) % major) * minor + (row_minor + minor_step) % minor

    peers = [(row_at(step, 0), col) for step in range(1, major)]
    peers += [(row_at(0, step), col) for step in range(1, minor)]
    peers += [(row, (col + step) % cols) for step in range(1, cols)]
    barrier = pltpu.get_barrier_semaphore()
    for peer in peers:
        pl.semaphore_signal(barrier, inc=1, device_id=peer, device_id_type=MESH)

    def lanes_of(chunk):
        return slice(chunk * lanes, (chunk + 1) * lanes)

    def plan(step):
        if step < levels - 1:
            return step, step + 1, 2, lower_source, lower_target, step == 0, list(range(step + 2, levels))
        source = 2 * (levels - 1) - step
        first = step == levels - 1
        return source - 1, source - 1, 4, upper_source, upper_target, first, list(range(source - 1))

    def far_slot(step, level):
        return level - 2 if step < levels - 1 else level

    pending = {}

    def push(step, chunk, slot, target, index, needed=None):
        ref = panels[step * CHUNKS + chunk]

        def make():
            return pltpu.make_async_remote_copy(
                src_ref=ref.at[slot],
                dst_ref=ref.at[slot],
                send_sem=gather_send.at[chunk, index],
                recv_sem=gather_recv.at[step, chunk, slot],
                device_id=(target, col),
                device_id_type=MESH,
            )

        pending.setdefault(("gather", step, chunk), []).append((make, needed))
        when(needed, lambda: make().start())

    def when(needed, action):
        if needed is None:
            action()
        else:
            pl.when(needed)(action)

    def arrived(step, chunk, slot):
        ref = panels[step * CHUNKS + chunk]
        pltpu.make_async_remote_copy(
            src_ref=ref.at[slot],
            dst_ref=ref.at[slot],
            send_sem=gather_send.at[chunk, 0],
            recv_sem=gather_recv.at[step, chunk, slot],
            device_id=(row, col),
            device_id_type=MESH,
        ).wait_recv()

    def drain(kind, step, chunk):
        for make, needed in pending.pop((kind, step, chunk), []):
            when(needed, lambda: make().wait_send())

    def gather_major(step, chunk):
        push(step, chunk, row, row + minor, 0, row_major + 1 < major)
        push(step, chunk, row, row - minor, 1, row_major >= 1)

    def gather_minor(step, chunk):
        for across in range(1, minor):
            push(step, chunk, row, row_at(0, across), 1 + across)

    def relay(step, chunk, hops):
        if hops >= major:
            return
        for side, sign in enumerate((-1, 1)):
            origin = row_major + sign * hops
            slot = row + sign * hops * minor
            came = (origin >= 0) & (origin < major)
            base = 1 + minor + ((hops - 1) * 2 + side) * minor
            when(came, lambda: arrived(step, chunk, slot))
            if hops + 1 < major:
                after = row_major - sign
                push(step, chunk, slot, row - sign * minor, base, came & (after >= 0) & (after < major))
            for across in range(1, minor):
                push(step, chunk, slot, row_at(0, across), base + across, came)

    def gather_finish(step, chunk):
        for across in range(1, minor):
            for offset in range(major):
                arrived(step, chunk, row_at(offset, across))

    def picked(target_ref, at, wanted):
        total = jnp.zeros((width, lanes), F32)
        for k in range(slots):
            mask = jnp.full((width, lanes), target_ref[at, 0, k], jnp.int32) == wanted
            total = total + jnp.where(mask, products[k], 0.0)
        return total

    def update_near(step, chunk):
        at, level, blocks, source, target, first, _ = plan(step)
        ref = panels[step * CHUNKS + chunk]
        held = load(blocks, at)
        for k in range(slots):
            products[k] = jnp.dot(held[k], ref[source[at, 0, k]], preferred_element_type=F32)
        drain("sum", step - 1, chunk)
        for offset in list(range(1, cols)) + [0]:
            owner = (col + offset) % cols
            total = picked(target, at, level * cols + owner)
            if not first:
                total = total + far[far_slot(step, level), owner, chunk]
            if offset == 0:
                owned[chunk] = total.astype(BF16)
                continue
            outbox[step, chunk, offset - 1] = total.astype(BF16)
            copy = pltpu.make_async_remote_copy(
                src_ref=outbox.at[step, chunk, offset - 1],
                dst_ref=inbox.at[step, chunk, offset - 1],
                send_sem=sum_send.at[chunk, offset - 1],
                recv_sem=sum_recv.at[step, chunk, offset - 1],
                device_id=(row, owner),
                device_id_type=MESH,
            )
            copy.start()
            pending.setdefault(("sum", step, chunk), []).append((lambda copy=copy: copy, None))

    def update_far(step, chunk):
        at, _, _, _, target, first, others = plan(step)
        for level in others:
            place = far_slot(step, level)

            @pl.loop(0, cols)
            def _(q):
                total = picked(target, at, level * cols + q)
                if not first:
                    total = total + far[place, q, chunk]
                far[place, q, chunk] = total

    def finish_sum(step, chunk):
        level = plan(step)[1]
        total = owned[chunk].astype(F32)
        for make, _ in pending[("sum", step, chunk)]:
            make().wait_recv()
        for offset in range(1, cols):
            total = total + inbox[step, chunk, offset - 1].astype(F32)
        if step < levels - 1:
            solve_lower(level, chunk, load(0, level)[0, :, lanes_of(chunk)].astype(F32) - total)
        else:
            solve_upper(level, chunk, forward[level, chunk] - total)

    def publish(step, chunk, result):
        if step < rounds:
            panels[step * CHUNKS + chunk][row] = result.astype(BF16)
            drain("gather", step - 1, chunk)

    def solve_lower(level, chunk, lowered):
        result = jnp.dot(load(1, level)[0], lowered.astype(BF16), preferred_element_type=F32)
        forward[level, chunk] = result
        if level == levels - 1:
            solve_upper(level, chunk, result)
        else:
            publish(level, chunk, result)

    def solve_upper(level, chunk, raised):
        result = jnp.dot(load(3, level)[0], raised.astype(BF16), preferred_element_type=F32)
        out_ref[level, 0, :, lanes_of(chunk)] = result
        if chunk == CHUNKS - 1:
            store(level).start()
        publish(2 * (levels - 1) - level, chunk, result)

    for ref, index in order:
        fetch(ref, index).start()
    for chunk in range(CHUNKS):
        solve_lower(0, chunk, load(0, 0)[0, :, lanes_of(chunk)].astype(F32))
    pl.semaphore_wait(barrier, len(peers))

    def turn(step, chunk, other_step):
        other = 1 - chunk

        def relay_other(hops):
            if other_step < rounds:
                relay(other_step, other, hops)

        gather_finish(step, chunk)
        update_near(step, chunk)
        relay_other(1)
        update_far(step, chunk)
        for hops in range(2, major - 1):
            relay_other(hops)
        finish_sum(step, chunk)
        if step + 1 < rounds:
            gather_major(step + 1, chunk)
        if major > 2:
            relay_other(major - 1)
        if step + 1 < rounds:
            gather_minor(step + 1, chunk)

    for chunk in range(CHUNKS):
        gather_major(0, chunk)
        gather_minor(0, chunk)
    for hops in range(1, major):
        relay(0, 0, hops)
    for step in range(rounds):
        turn(step, 0, step)
        turn(step, 1, step + 1)
    for kind in ("gather", "sum"):
        for chunk in range(CHUNKS):
            drain(kind, rounds - 1, chunk)
    for level in range(levels):
        store(level).wait()


def shards(*args):
    rows, cols = lax.axis_size("row"), lax.axis_size("col")
    levels, per_device, width, rhs_cols = args[0].shape
    slots = args[1].shape[3]
    assert per_device == 1 and rhs_cols % CHUNKS == 0 and levels > 2
    lanes = rhs_cols // CHUNKS
    rounds = 2 * (levels - 1)
    major = 4 if rows % 4 == 0 else 1
    minor = rows // major
    copies = 1 + minor + 2 * (major - 1) * minor
    smem = pl.BlockSpec(memory_space=pltpu.SMEM)
    anywhere = pl.BlockSpec(memory_space=pl.ANY)
    args = [arg.reshape(levels - 1, 1, slots) if arg.dtype == jnp.int32 else arg for arg in args]
    scratch = [pltpu.VMEM((rows, width, lanes), BF16) for _ in range(rounds * CHUNKS)]
    scratch += [
        pltpu.VMEM((levels, CHUNKS, width, lanes), F32),
        pltpu.VMEM((levels - 2, cols, CHUNKS, width, lanes), F32),
        pltpu.VMEM((slots, width, lanes), F32),
        pltpu.VMEM((CHUNKS, width, lanes), BF16),
        pltpu.VMEM((rounds, CHUNKS, cols - 1, width, lanes), BF16),
        pltpu.VMEM((rounds, CHUNKS, cols - 1, width, lanes), BF16),
        pltpu.SemaphoreType.DMA((CHUNKS, copies)),
        pltpu.SemaphoreType.DMA((rounds, CHUNKS, rows)),
        pltpu.SemaphoreType.DMA((CHUNKS, cols - 1)),
        pltpu.SemaphoreType.DMA((rounds, CHUNKS, cols - 1)),
    ]
    scratch += [pltpu.VMEM(args[i].shape[-4:], BF16) for i in (0, 4)]
    scratch += [pltpu.VMEM(args[1].shape[-4:], BF16)]
    scratch += [pltpu.VMEM(args[8].shape, BF16), pltpu.VMEM(args[5].shape[-4:], BF16)]
    scratch += [
        pltpu.VMEM(args[0].shape, F32),
        pltpu.SemaphoreType.DMA((5, levels)),
        pltpu.SemaphoreType.DMA((levels,)),
    ]
    return pl.pallas_call(
        functools.partial(kernel, rows, cols, levels, slots, width, lanes),
        out_shape=jax.ShapeDtypeStruct(args[0].shape, F32),
        in_specs=[anywhere, anywhere, smem, smem, anywhere, anywhere, smem, smem, anywhere],
        out_specs=anywhere,
        scratch_shapes=scratch,
        compiler_params=pltpu.CompilerParams(
            collective_id=0, has_side_effects=True, vmem_limit_bytes=60 * 1024 * 1024
        ),
    )(*args)


def solution(mesh):
    in_specs = (
        P(None, ("row", "col"), None, None),
        P("row", "col", None, None, None, None),
        P("row", "col", None, None),
        P("row", "col", None, None),
        P(None, ("row", "col"), None, None),
        P("row", "col", None, None, None, None),
        P("row", "col", None, None),
        P("row", "col", None, None),
        P(None, ("row", "col"), None, None),
    )
    out_specs = P(None, ("row", "col"), None, None)
    return jax.shard_map(shards, mesh=mesh, in_specs=in_specs, out_specs=out_specs, check_vma=False)
```

```python
import functools

import jax
import jax.numpy as jnp
from jax import lax
from jax.experimental import pallas as pl
from jax.experimental.pallas import tpu as pltpu
from jax.sharding import PartitionSpec as P

MESH = pl.DeviceIdType.MESH
CHUNKS = 2
F32 = jnp.float32
BF16 = jnp.bfloat16


def kernel(
    rows,
    cols,
    levels,
    slots,
    width,
    lanes,
    rhs_hbm,
    lower_hbm,
    lower_source,
    lower_target,
    diag_lower_hbm,
    upper_hbm,
    upper_source,
    upper_target,
    diag_upper_hbm,
    out_hbm,
    *scratch,
):
    rounds = 2 * (levels - 1)
    panels = scratch[: rounds * CHUNKS]
    rest = scratch[rounds * CHUNKS :]
    forward, far, products, owned, outbox, inbox, gather_send, gather_recv, sum_send, sum_recv = rest[:10]
    inputs, out_ref, load_sem, store_sem = rest[10:15], rest[15], rest[16], rest[17]
    sources = (rhs_hbm, diag_lower_hbm, lower_hbm.at[0, 0], diag_upper_hbm, upper_hbm.at[0, 0])
    order = [(0, 0), (1, 0), (2, 0)]
    for level in range(1, levels):
        order += [(0, level), (1, level)] + ([(2, level)] if level < levels - 1 else [])
    for level in range(levels - 1, -1, -1):
        order += [(3, level)] + ([(4, level - 1)] if level else [])
    loaded = set()

    def fetch(ref, index):
        return pltpu.make_async_copy(sources[ref].at[index], inputs[ref].at[index], load_sem.at[ref, index])

    def load(ref, index):
        if (ref, index) not in loaded:
            loaded.add((ref, index))
            fetch(ref, index).wait()
        return inputs[ref].at[index]

    def store(level):
        return pltpu.make_async_copy(out_ref.at[level], out_hbm.at[level], store_sem.at[level])

    major = 4 if rows % 4 == 0 else 1
    minor = rows // major
    row, col = lax.axis_index("row"), lax.axis_index("col")
    row_major, row_minor = row // minor, row % minor

    def row_at(major_step, minor_step):
        return ((row_major + major_step) % major) * minor + (row_minor + minor_step) % minor

    peers = [(row_at(step, 0), col) for step in range(1, major)]
    peers += [(row_at(0, step), col) for step in range(1, minor)]
    peers += [(row, (col + step) % cols) for step in range(1, cols)]
    barrier = pltpu.get_barrier_semaphore()
    for peer in peers:
        pl.semaphore_signal(barrier, inc=1, device_id=peer, device_id_type=MESH)

    def lanes_of(chunk):
        return slice(chunk * lanes, (chunk + 1) * lanes)

    def plan(step):
        if step < levels - 1:
            return step, step + 1, 2, lower_source, lower_target, step == 0, list(range(step + 2, levels))
        source = 2 * (levels - 1) - step
        first = step == levels - 1
        return source - 1, source - 1, 4, upper_source, upper_target, first, list(range(source - 1))

    def far_slot(step, level):
        return level - 2 if step < levels - 1 else level

    pending = {}

    def push(step, chunk, slot, target, index, needed=None):
        ref = panels[step * CHUNKS + chunk]

        def make():
            return pltpu.make_async_remote_copy(
                src_ref=ref.at[slot],
                dst_ref=ref.at[slot],
                send_sem=gather_send.at[chunk, index],
                recv_sem=gather_recv.at[step, chunk, slot],
                device_id=(target, col),
                device_id_type=MESH,
            )

        pending.setdefault(("gather", step, chunk), []).append((make, needed))
        when(needed, lambda: make().start())

    def when(needed, action):
        if needed is None:
            action()
        else:
            pl.when(needed)(action)

    def arrived(step, chunk, slot):
        ref = panels[step * CHUNKS + chunk]
        pltpu.make_async_remote_copy(
            src_ref=ref.at[slot],
            dst_ref=ref.at[slot],
            send_sem=gather_send.at[chunk, 0],
            recv_sem=gather_recv.at[step, chunk, slot],
            device_id=(row, col),
            device_id_type=MESH,
        ).wait_recv()

    def drain(kind, step, chunk):
        for make, needed in pending.pop((kind, step, chunk), []):
            when(needed, lambda: make().wait_send())

    def gather_major(step, chunk):
        for hops in range(1, major):
            push(step, chunk, row, row + hops * minor, 2 * hops - 2, row_major + hops < major)
            push(step, chunk, row, row - hops * minor, 2 * hops - 1, row_major >= hops)

    def gather_minor(step, chunk):
        for across in range(1, minor):
            push(step, chunk, row, row_at(0, across), 2 * major - 3 + across)

    def relay(step, chunk, hops):
        for side, sign in enumerate((-1, 1)):
            origin = row_major + sign * hops
            slot = row + sign * hops * minor
            came = (origin >= 0) & (origin < major)
            base = 2 * major - 3 + minor + (2 * hops - 2 + side) * (minor - 1)
            when(came, lambda: arrived(step, chunk, slot))
            for across in range(1, minor):
                push(step, chunk, slot, row_at(0, across), base + across - 1, came)

    def gather_finish(step, chunk):
        for across in range(1, minor):
            for offset in range(major):
                arrived(step, chunk, row_at(offset, across))

    def picked(target_ref, at, wanted):
        total = jnp.zeros((width, lanes), F32)
        for k in range(slots):
            mask = jnp.full((width, lanes), target_ref[at, 0, k], jnp.int32) == wanted
            total = total + jnp.where(mask, products[k], 0.0)
        return total

    def update_near(step, chunk):
        at, level, blocks, source, target, first, _ = plan(step)
        ref = panels[step * CHUNKS + chunk]
        held = load(blocks, at)
        for k in range(slots):
            products[k] = jnp.dot(held[k], ref[source[at, 0, k]], preferred_element_type=F32)
        drain("sum", step - 1, chunk)
        for offset in list(range(1, cols)) + [0]:
            owner = (col + offset) % cols
            total = picked(target, at, level * cols + owner)
            if not first:
                total = total + far[far_slot(step, level), owner, chunk]
            if offset == 0:
                owned[chunk] = total.astype(BF16)
                continue
            outbox[step, chunk, offset - 1] = total.astype(BF16)
            copy = pltpu.make_async_remote_copy(
                src_ref=outbox.at[step, chunk, offset - 1],
                dst_ref=inbox.at[step, chunk, offset - 1],
                send_sem=sum_send.at[chunk, offset - 1],
                recv_sem=sum_recv.at[step, chunk, offset - 1],
                device_id=(row, owner),
                device_id_type=MESH,
            )
            copy.start()
            pending.setdefault(("sum", step, chunk), []).append((lambda copy=copy: copy, None))

    def update_far(step, chunk):
        at, _, _, _, target, first, others = plan(step)
        for level in others:
            place = far_slot(step, level)

            @pl.loop(0, cols)
            def _(q):
                total = picked(target, at, level * cols + q)
                if not first:
                    total = total + far[place, q, chunk]
                far[place, q, chunk] = total

    def finish_sum(step, chunk):
        level = plan(step)[1]
        total = owned[chunk].astype(F32)
        for make, _ in pending[("sum", step, chunk)]:
            make().wait_recv()
        for offset in range(1, cols):
            total = total + inbox[step, chunk, offset - 1].astype(F32)
        if step < levels - 1:
            solve_lower(level, chunk, load(0, level)[0, :, lanes_of(chunk)].astype(F32) - total)
        else:
            solve_upper(level, chunk, forward[level, chunk] - total)

    def publish(step, chunk, result):
        if step < rounds:
            panels[step * CHUNKS + chunk][row] = result.astype(BF16)
            drain("gather", step - 1, chunk)

    def solve_lower(level, chunk, lowered):
        result = jnp.dot(load(1, level)[0], lowered.astype(BF16), preferred_element_type=F32)
        forward[level, chunk] = result
        if level == levels - 1:
            solve_upper(level, chunk, result)
        else:
            publish(level, chunk, result)

    def solve_upper(level, chunk, raised):
        result = jnp.dot(load(3, level)[0], raised.astype(BF16), preferred_element_type=F32)
        out_ref[level, 0, :, lanes_of(chunk)] = result
        if chunk == CHUNKS - 1:
            store(level).start()
        publish(2 * (levels - 1) - level, chunk, result)

    for ref, index in order:
        fetch(ref, index).start()
    for chunk in range(CHUNKS):
        solve_lower(0, chunk, load(0, 0)[0, :, lanes_of(chunk)].astype(F32))
    pl.semaphore_wait(barrier, len(peers))

    def turn(step, chunk, other_step):
        other = 1 - chunk

        def relay_other(hops):
            if other_step < rounds and hops < major:
                relay(other_step, other, hops)

        gather_finish(step, chunk)
        relay_other(1)
        update_near(step, chunk)
        relay_other(2)
        update_far(step, chunk)
        for hops in range(3, major):
            relay_other(hops)
        finish_sum(step, chunk)
        if step + 1 < rounds:
            gather_minor(step + 1, chunk)
            gather_major(step + 1, chunk)

    gather_minor(0, 0)
    gather_major(0, 0)
    for hops in range(1, major):
        relay(0, 0, hops)
        if hops == 1:
            gather_minor(0, 1)
            gather_major(0, 1)
    for step in range(rounds):
        turn(step, 0, step)
        turn(step, 1, step + 1)
    for kind in ("gather", "sum"):
        for chunk in range(CHUNKS):
            drain(kind, rounds - 1, chunk)
    for level in range(levels):
        store(level).wait()


def shards(*args):
    rows, cols = lax.axis_size("row"), lax.axis_size("col")
    levels, per_device, width, rhs_cols = args[0].shape
    slots = args[1].shape[3]
    assert per_device == 1 and rhs_cols % CHUNKS == 0 and levels > 2
    lanes = rhs_cols // CHUNKS
    rounds = 2 * (levels - 1)
    major = 4 if rows % 4 == 0 else 1
    minor = rows // major
    copies = 2 * major - 2 + minor - 1 + 2 * (major - 1) * (minor - 1)
    smem = pl.BlockSpec(memory_space=pltpu.SMEM)
    anywhere = pl.BlockSpec(memory_space=pl.ANY)
    args = [arg.reshape(levels - 1, 1, slots) if arg.dtype == jnp.int32 else arg for arg in args]
    scratch = [pltpu.VMEM((rows, width, lanes), BF16) for _ in range(rounds * CHUNKS)]
    scratch += [
        pltpu.VMEM((levels, CHUNKS, width, lanes), F32),
        pltpu.VMEM((levels - 2, cols, CHUNKS, width, lanes), F32),
        pltpu.VMEM((slots, width, lanes), F32),
        pltpu.VMEM((CHUNKS, width, lanes), BF16),
        pltpu.VMEM((rounds, CHUNKS, cols - 1, width, lanes), BF16),
        pltpu.VMEM((rounds, CHUNKS, cols - 1, width, lanes), BF16),
        pltpu.SemaphoreType.DMA((CHUNKS, copies)),
        pltpu.SemaphoreType.DMA((rounds, CHUNKS, rows)),
        pltpu.SemaphoreType.DMA((CHUNKS, cols - 1)),
        pltpu.SemaphoreType.DMA((rounds, CHUNKS, cols - 1)),
    ]
    scratch += [pltpu.VMEM(args[i].shape[-4:], BF16) for i in (0, 4)]
    scratch += [pltpu.VMEM(args[1].shape[-4:], BF16)]
    scratch += [pltpu.VMEM(args[8].shape, BF16), pltpu.VMEM(args[5].shape[-4:], BF16)]
    scratch += [
        pltpu.VMEM(args[0].shape, F32),
        pltpu.SemaphoreType.DMA((5, levels)),
        pltpu.SemaphoreType.DMA((levels,)),
    ]
    return pl.pallas_call(
        functools.partial(kernel, rows, cols, levels, slots, width, lanes),
        out_shape=jax.ShapeDtypeStruct(args[0].shape, F32),
        in_specs=[anywhere, anywhere, smem, smem, anywhere, anywhere, smem, smem, anywhere],
        out_specs=anywhere,
        scratch_shapes=scratch,
        compiler_params=pltpu.CompilerParams(
            collective_id=0, has_side_effects=True, vmem_limit_bytes=60 * 1024 * 1024
        ),
    )(*args)


def solution(mesh):
    in_specs = (
        P(None, ("row", "col"), None, None),
        P("row", "col", None, None, None, None),
        P("row", "col", None, None),
        P("row", "col", None, None),
        P(None, ("row", "col"), None, None),
        P("row", "col", None, None, None, None),
        P("row", "col", None, None),
        P("row", "col", None, None),
        P(None, ("row", "col"), None, None),
    )
    out_specs = P(None, ("row", "col"), None, None)
    return jax.shard_map(shards, mesh=mesh, in_specs=in_specs, out_specs=out_specs, check_vma=False)
```

```python
import functools

import jax
import jax.numpy as jnp
from jax import lax
from jax.experimental import pallas as pl
from jax.experimental.pallas import tpu as pltpu
from jax.sharding import PartitionSpec as P

MESH = pl.DeviceIdType.MESH
CHUNKS = 2
F32 = jnp.float32
BF16 = jnp.bfloat16


def kernel(
    rows,
    cols,
    levels,
    slots,
    width,
    lanes,
    rhs_hbm,
    lower_hbm,
    lower_source,
    lower_target,
    diag_lower_hbm,
    upper_hbm,
    upper_source,
    upper_target,
    diag_upper_hbm,
    out_hbm,
    *scratch,
):
    rounds = 2 * (levels - 1)
    panels = scratch[: rounds * CHUNKS]
    rest = scratch[rounds * CHUNKS :]
    forward, far, sums, owned, outbox, inbox, gather_send, gather_recv, sum_send, sum_recv = rest[:10]
    inputs, out_ref, load_sem, store_sem = rest[10:15], rest[15], rest[16], rest[17]
    sources = (rhs_hbm, diag_lower_hbm, lower_hbm.at[0, 0], diag_upper_hbm, upper_hbm.at[0, 0])
    order = [(0, 0), (1, 0), (2, 0)]
    for level in range(1, levels):
        order += [(0, level), (1, level)] + ([(2, level)] if level < levels - 1 else [])
    for level in range(levels - 1, -1, -1):
        order += [(3, level)] + ([(4, level - 1)] if level else [])
    loaded = set()

    def fetch(ref, index):
        return pltpu.make_async_copy(sources[ref].at[index], inputs[ref].at[index], load_sem.at[ref, index])

    def load(ref, index):
        if (ref, index) not in loaded:
            loaded.add((ref, index))
            fetch(ref, index).wait()
        return inputs[ref].at[index]

    def store(level):
        return pltpu.make_async_copy(out_ref.at[level], out_hbm.at[level], store_sem.at[level])

    major = 4 if rows % 4 == 0 else 1
    minor = rows // major
    row, col = lax.axis_index("row"), lax.axis_index("col")
    row_major, row_minor = row // minor, row % minor

    def row_at(major_step, minor_step):
        return ((row_major + major_step) % major) * minor + (row_minor + minor_step) % minor

    peers = [(row_at(step, 0), col) for step in range(1, major)]
    peers += [(row_at(0, step), col) for step in range(1, minor)]
    peers += [(row, (col + step) % cols) for step in range(1, cols)]
    barrier = pltpu.get_barrier_semaphore()
    for peer in peers:
        pl.semaphore_signal(barrier, inc=1, device_id=peer, device_id_type=MESH)

    def lanes_of(chunk):
        return slice(chunk * lanes, (chunk + 1) * lanes)

    def plan(step):
        if step < levels - 1:
            return step, step + 1, 2, lower_source, lower_target, step == 0, list(range(step + 2, levels))
        source = 2 * (levels - 1) - step
        first = step == levels - 1
        return source - 1, source - 1, 4, upper_source, upper_target, first, list(range(source - 1))

    def far_slot(step, level):
        return level - 2 if step < levels - 1 else level

    pending = {}

    def push(step, chunk, slot, target, index, needed=None):
        ref = panels[step * CHUNKS + chunk]

        def make():
            return pltpu.make_async_remote_copy(
                src_ref=ref.at[slot],
                dst_ref=ref.at[slot],
                send_sem=gather_send.at[chunk, index],
                recv_sem=gather_recv.at[step, chunk, slot],
                device_id=(target, col),
                device_id_type=MESH,
            )

        pending.setdefault(("gather", step, chunk), []).append((make, needed))
        when(needed, lambda: make().start())

    def when(needed, action):
        if needed is None:
            action()
        else:
            pl.when(needed)(action)

    def arrived(step, chunk, slot):
        ref = panels[step * CHUNKS + chunk]
        pltpu.make_async_remote_copy(
            src_ref=ref.at[slot],
            dst_ref=ref.at[slot],
            send_sem=gather_send.at[chunk, 0],
            recv_sem=gather_recv.at[step, chunk, slot],
            device_id=(row, col),
            device_id_type=MESH,
        ).wait_recv()

    def drain(kind, step, chunk):
        for make, needed in pending.pop((kind, step, chunk), []):
            when(needed, lambda: make().wait_send())

    def gather_major(step, chunk):
        push(step, chunk, row, row + minor, 0, row_major + 1 < major)
        push(step, chunk, row, row - minor, 1, row_major >= 1)

    def gather_minor(step, chunk):
        for across in range(1, minor):
            push(step, chunk, row, row_at(0, across), 1 + across)

    def relay(step, chunk, hops):
        if hops >= major:
            return
        for side, sign in enumerate((-1, 1)):
            origin = row_major + sign * hops
            slot = row + sign * hops * minor
            came = (origin >= 0) & (origin < major)
            base = 1 + minor + ((hops - 1) * 2 + side) * minor
            when(came, lambda: arrived(step, chunk, slot))
            if hops + 1 < major:
                after = row_major - sign
                push(step, chunk, slot, row - sign * minor, base, came & (after >= 0) & (after < major))
            for across in range(1, minor):
                push(step, chunk, slot, row_at(0, across), base + across, came)

    def gather_finish(step, chunk):
        for across in range(1, minor):
            for offset in range(major):
                arrived(step, chunk, row_at(offset, across))

    def last_slot(target, at, wanted, before):
        found = jnp.int32(slots)
        for k in range(before):
            found = jnp.where(target[at, 0, k] == wanted, k, found)
        return found

    def update_near(step, chunk):
        at, level, blocks, source, target, first, _ = plan(step)
        ref = panels[step * CHUNKS + chunk]
        held = load(blocks, at)
        for k in range(slots):
            total = jnp.dot(held[k], ref[source[at, 0, k]], preferred_element_type=F32)
            if k > 0:
                total = total + sums[last_slot(target, at, target[at, 0, k], k)]
            sums[k] = total
        drain("sum", step - 1, chunk)
        for offset in list(range(1, cols)) + [0]:
            owner = (col + offset) % cols
            total = sums[last_slot(target, at, level * cols + owner, slots)]
            if not first:
                total = total + far[far_slot(step, level), owner, chunk]
            if offset == 0:
                owned[chunk] = total.astype(BF16)
                continue
            outbox[step, chunk, offset - 1] = total.astype(BF16)
            copy = pltpu.make_async_remote_copy(
                src_ref=outbox.at[step, chunk, offset - 1],
                dst_ref=inbox.at[step, chunk, offset - 1],
                send_sem=sum_send.at[chunk, offset - 1],
                recv_sem=sum_recv.at[step, chunk, offset - 1],
                device_id=(row, owner),
                device_id_type=MESH,
            )
            copy.start()
            pending.setdefault(("sum", step, chunk), []).append((lambda copy=copy: copy, None))

    def update_far(step, chunk):
        at, _, _, _, target, first, others = plan(step)
        for level in others:
            place = far_slot(step, level)

            @pl.loop(0, cols)
            def _(q):
                total = sums[last_slot(target, at, level * cols + q, slots)]
                if not first:
                    total = total + far[place, q, chunk]
                far[place, q, chunk] = total

    def finish_sum(step, chunk):
        level = plan(step)[1]
        total = owned[chunk].astype(F32)
        for make, _ in pending[("sum", step, chunk)]:
            make().wait_recv()
        for offset in range(1, cols):
            total = total + inbox[step, chunk, offset - 1].astype(F32)
        if step < levels - 1:
            solve_lower(level, chunk, load(0, level)[0, :, lanes_of(chunk)].astype(F32) - total)
        else:
            solve_upper(level, chunk, forward[level, chunk] - total)

    def publish(step, chunk, result):
        if step < rounds:
            panels[step * CHUNKS + chunk][row] = result.astype(BF16)
            drain("gather", step - 1, chunk)

    def solve_lower(level, chunk, lowered):
        result = jnp.dot(load(1, level)[0], lowered.astype(BF16), preferred_element_type=F32)
        forward[level, chunk] = result
        if level == levels - 1:
            solve_upper(level, chunk, result)
        else:
            publish(level, chunk, result)

    def solve_upper(level, chunk, raised):
        result = jnp.dot(load(3, level)[0], raised.astype(BF16), preferred_element_type=F32)
        out_ref[level, 0, :, lanes_of(chunk)] = result
        if chunk == CHUNKS - 1:
            store(level).start()
        publish(2 * (levels - 1) - level, chunk, result)

    for ref, index in order:
        fetch(ref, index).start()
    sums[slots] = jnp.zeros((width, lanes), F32)
    for chunk in range(CHUNKS):
        solve_lower(0, chunk, load(0, 0)[0, :, lanes_of(chunk)].astype(F32))
    pl.semaphore_wait(barrier, len(peers))

    def turn(step, chunk, other_step):
        other = 1 - chunk

        def relay_other(hops):
            if other_step < rounds and hops < major:
                relay(other_step, other, hops)

        gather_finish(step, chunk)
        relay_other(1)
        update_near(step, chunk)
        relay_other(2)
        update_far(step, chunk)
        for hops in range(3, major):
            relay_other(hops)
        finish_sum(step, chunk)
        if step + 1 < rounds:
            gather_major(step + 1, chunk)
            gather_minor(step + 1, chunk)

    gather_major(0, 0)
    gather_minor(0, 0)
    for hops in range(1, major):
        relay(0, 0, hops)
        if hops == 1:
            gather_major(0, 1)
            gather_minor(0, 1)
    for step in range(rounds):
        turn(step, 0, step)
        turn(step, 1, step + 1)
    for kind in ("gather", "sum"):
        for chunk in range(CHUNKS):
            drain(kind, rounds - 1, chunk)
    for level in range(levels):
        store(level).wait()


def shards(*args):
    rows, cols = lax.axis_size("row"), lax.axis_size("col")
    levels, per_device, width, rhs_cols = args[0].shape
    slots = args[1].shape[3]
    assert per_device == 1 and rhs_cols % CHUNKS == 0 and levels > 2
    lanes = rhs_cols // CHUNKS
    rounds = 2 * (levels - 1)
    major = 4 if rows % 4 == 0 else 1
    minor = rows // major
    copies = 1 + minor + 2 * (major - 1) * minor
    smem = pl.BlockSpec(memory_space=pltpu.SMEM)
    anywhere = pl.BlockSpec(memory_space=pl.ANY)
    args = [arg.reshape(levels - 1, 1, slots) if arg.dtype == jnp.int32 else arg for arg in args]
    scratch = [pltpu.VMEM((rows, width, lanes), BF16) for _ in range(rounds * CHUNKS)]
    scratch += [
        pltpu.VMEM((levels, CHUNKS, width, lanes), F32),
        pltpu.VMEM((levels - 2, cols, CHUNKS, width, lanes), F32),
        pltpu.VMEM((slots + 1, width, lanes), F32),
        pltpu.VMEM((CHUNKS, width, lanes), BF16),
        pltpu.VMEM((rounds, CHUNKS, cols - 1, width, lanes), BF16),
        pltpu.VMEM((rounds, CHUNKS, cols - 1, width, lanes), BF16),
        pltpu.SemaphoreType.DMA((CHUNKS, copies)),
        pltpu.SemaphoreType.DMA((rounds, CHUNKS, rows)),
        pltpu.SemaphoreType.DMA((CHUNKS, cols - 1)),
        pltpu.SemaphoreType.DMA((rounds, CHUNKS, cols - 1)),
    ]
    scratch += [pltpu.VMEM(args[i].shape[-4:], BF16) for i in (0, 4)]
    scratch += [pltpu.VMEM(args[1].shape[-4:], BF16)]
    scratch += [pltpu.VMEM(args[8].shape, BF16), pltpu.VMEM(args[5].shape[-4:], BF16)]
    scratch += [
        pltpu.VMEM(args[0].shape, F32),
        pltpu.SemaphoreType.DMA((5, levels)),
        pltpu.SemaphoreType.DMA((levels,)),
    ]
    return pl.pallas_call(
        functools.partial(kernel, rows, cols, levels, slots, width, lanes),
        out_shape=jax.ShapeDtypeStruct(args[0].shape, F32),
        in_specs=[anywhere, anywhere, smem, smem, anywhere, anywhere, smem, smem, anywhere],
        out_specs=anywhere,
        scratch_shapes=scratch,
        compiler_params=pltpu.CompilerParams(
            collective_id=0, has_side_effects=True, vmem_limit_bytes=60 * 1024 * 1024
        ),
    )(*args)


def solution(mesh):
    in_specs = (
        P(None, ("row", "col"), None, None),
        P("row", "col", None, None, None, None),
        P("row", "col", None, None),
        P("row", "col", None, None),
        P(None, ("row", "col"), None, None),
        P("row", "col", None, None, None, None),
        P("row", "col", None, None),
        P("row", "col", None, None),
        P(None, ("row", "col"), None, None),
    )
    out_specs = P(None, ("row", "col"), None, None)
    return jax.shard_map(shards, mesh=mesh, in_specs=in_specs, out_specs=out_specs, check_vma=False)
```

```python
import functools

import jax
import jax.numpy as jnp
from jax import lax
from jax.experimental import pallas as pl
from jax.experimental.pallas import tpu as pltpu
from jax.sharding import PartitionSpec as P

MESH = pl.DeviceIdType.MESH
CHUNKS = 2
F32 = jnp.float32
BF16 = jnp.bfloat16


def kernel(
    rows,
    cols,
    levels,
    slots,
    width,
    lanes,
    rhs_hbm,
    lower_hbm,
    lower_source,
    lower_target,
    diag_lower_hbm,
    upper_hbm,
    upper_source,
    upper_target,
    diag_upper_hbm,
    out_hbm,
    *scratch,
):
    rounds = 2 * (levels - 1)
    panels = scratch[: rounds * CHUNKS]
    rest = scratch[rounds * CHUNKS :]
    forward, far, sums, owned, outbox, inbox, gather_send, gather_recv, sum_send, sum_recv = rest[:10]
    inputs, out_ref, load_sem, store_sem = rest[10:15], rest[15], rest[16], rest[17]
    sources = (rhs_hbm, diag_lower_hbm, lower_hbm.at[0, 0], diag_upper_hbm, upper_hbm.at[0, 0])
    order = [(0, 0), (1, 0), (2, 0)]
    for level in range(1, levels):
        order += [(0, level), (1, level)] + ([(2, level)] if level < levels - 1 else [])
    for level in range(levels - 1, -1, -1):
        order += [(3, level)] + ([(4, level - 1)] if level else [])
    loaded = set()

    def fetch(ref, index):
        return pltpu.make_async_copy(sources[ref].at[index], inputs[ref].at[index], load_sem.at[ref, index])

    def load(ref, index):
        if (ref, index) not in loaded:
            loaded.add((ref, index))
            fetch(ref, index).wait()
        return inputs[ref].at[index]

    def store(level):
        return pltpu.make_async_copy(out_ref.at[level], out_hbm.at[level], store_sem.at[level])

    major = 4 if rows % 4 == 0 else 1
    minor = rows // major
    row, col = lax.axis_index("row"), lax.axis_index("col")
    row_major, row_minor = row // minor, row % minor

    def row_at(major_step, minor_step):
        return ((row_major + major_step) % major) * minor + (row_minor + minor_step) % minor

    peers = [(row_at(step, 0), col) for step in range(1, major)]
    peers += [(row_at(0, step), col) for step in range(1, minor)]
    peers += [(row, (col + step) % cols) for step in range(1, cols)]
    barrier = pltpu.get_barrier_semaphore()
    for peer in peers:
        pl.semaphore_signal(barrier, inc=1, device_id=peer, device_id_type=MESH)

    def lanes_of(chunk):
        return slice(chunk * lanes, (chunk + 1) * lanes)

    def plan(step):
        if step < levels - 1:
            return step, step + 1, 2, lower_source, lower_target, step == 0, list(range(step + 2, levels))
        source = 2 * (levels - 1) - step
        first = step == levels - 1
        return source - 1, source - 1, 4, upper_source, upper_target, first, list(range(source - 1))

    def far_slot(step, level):
        return level - 2 if step < levels - 1 else level

    pending = {}

    def push(step, chunk, slot, target, index, needed=None):
        ref = panels[step * CHUNKS + chunk]

        def make():
            return pltpu.make_async_remote_copy(
                src_ref=ref.at[slot],
                dst_ref=ref.at[slot],
                send_sem=gather_send.at[chunk, index],
                recv_sem=gather_recv.at[step, chunk, slot],
                device_id=(target, col),
                device_id_type=MESH,
            )

        pending.setdefault(("gather", step, chunk), []).append((make, needed))
        when(needed, lambda: make().start())

    def when(needed, action):
        if needed is None:
            action()
        else:
            pl.when(needed)(action)

    def arrived(step, chunk, slot):
        ref = panels[step * CHUNKS + chunk]
        pltpu.make_async_remote_copy(
            src_ref=ref.at[slot],
            dst_ref=ref.at[slot],
            send_sem=gather_send.at[chunk, 0],
            recv_sem=gather_recv.at[step, chunk, slot],
            device_id=(row, col),
            device_id_type=MESH,
        ).wait_recv()

    def drain(kind, step, chunk):
        for make, needed in pending.pop((kind, step, chunk), []):
            when(needed, lambda: make().wait_send())

    longest = major - 1
    at_end = (row_major == 0) | (row_major == longest)
    opposite = (longest - row_major) * minor + row_minor
    forwarded = 2 + minor

    def gather_major(step, chunk):
        push(step, chunk, row, row + minor, 0, row_major < longest)
        push(step, chunk, row, row - minor, 1, row_major > 0)
        if longest > 1:
            push(step, chunk, row, opposite, 2, at_end)

    def gather_minor(step, chunk):
        for across in range(1, minor):
            push(step, chunk, row, row_at(0, across), 1 + across)

    def cross(step, chunk):
        for across in range(1, minor):
            slot = row_at(0, across)
            arrived(step, chunk, slot)
            if longest > 1:
                push(step, chunk, slot, opposite, forwarded + across - 1, at_end)

    def relay(step, chunk, hops):
        for side, sign in enumerate((-1, 1)):
            origin = row_major + sign * hops
            slot = row + sign * hops * minor
            came = (origin >= 0) & (origin < major)
            base = forwarded + minor - 1 + ((hops - 1) * 2 + side) * minor
            when(came, lambda: arrived(step, chunk, slot))
            if hops + 1 < max(longest, 2):
                after = row_major - sign
                push(step, chunk, slot, row - sign * minor, base, came & (after >= 0) & (after < major))
            for across in range(1, minor):
                push(step, chunk, slot, row_at(0, across), base + across, came)

    def gather_finish(step, chunk):
        if longest > 1:
            when(at_end, lambda: arrived(step, chunk, opposite))
        for across in range(1, minor):
            for offset in range(1, major):
                arrived(step, chunk, row_at(offset, across))

    def last_slot(target, at, wanted, before):
        found = jnp.int32(slots)
        for k in range(before):
            found = jnp.where(target[at, 0, k] == wanted, k, found)
        return found

    def update_near(step, chunk):
        at, level, blocks, source, target, first, _ = plan(step)
        ref = panels[step * CHUNKS + chunk]
        held = load(blocks, at)
        for k in range(slots):
            total = jnp.dot(held[k], ref[source[at, 0, k]], preferred_element_type=F32)
            if k > 0:
                total = total + sums[last_slot(target, at, target[at, 0, k], k)]
            sums[k] = total
        drain("sum", step - 1, chunk)
        for offset in list(range(1, cols)) + [0]:
            owner = (col + offset) % cols
            total = sums[last_slot(target, at, level * cols + owner, slots)]
            if not first:
                total = total + far[far_slot(step, level), owner, chunk]
            if offset == 0:
                owned[chunk] = total.astype(BF16)
                continue
            outbox[step, chunk, offset - 1] = total.astype(BF16)
            copy = pltpu.make_async_remote_copy(
                src_ref=outbox.at[step, chunk, offset - 1],
                dst_ref=inbox.at[step, chunk, offset - 1],
                send_sem=sum_send.at[chunk, offset - 1],
                recv_sem=sum_recv.at[step, chunk, offset - 1],
                device_id=(row, owner),
                device_id_type=MESH,
            )
            copy.start()
            pending.setdefault(("sum", step, chunk), []).append((lambda copy=copy: copy, None))

    def update_far(step, chunk):
        at, _, _, _, target, first, others = plan(step)
        for level in others:
            place = far_slot(step, level)

            @pl.loop(0, cols)
            def _(q):
                total = sums[last_slot(target, at, level * cols + q, slots)]
                if not first:
                    total = total + far[place, q, chunk]
                far[place, q, chunk] = total

    def finish_sum(step, chunk):
        level = plan(step)[1]
        total = owned[chunk].astype(F32)
        for make, _ in pending[("sum", step, chunk)]:
            make().wait_recv()
        for offset in range(1, cols):
            total = total + inbox[step, chunk, offset - 1].astype(F32)
        if step < levels - 1:
            solve_lower(level, chunk, load(0, level)[0, :, lanes_of(chunk)].astype(F32) - total)
        else:
            solve_upper(level, chunk, forward[level, chunk] - total)

    def publish(step, chunk, result):
        if step < rounds:
            panels[step * CHUNKS + chunk][row] = result.astype(BF16)
            drain("gather", step - 1, chunk)

    def solve_lower(level, chunk, lowered):
        result = jnp.dot(load(1, level)[0], lowered.astype(BF16), preferred_element_type=F32)
        forward[level, chunk] = result
        if level == levels - 1:
            solve_upper(level, chunk, result)
        else:
            publish(level, chunk, result)

    def solve_upper(level, chunk, raised):
        result = jnp.dot(load(3, level)[0], raised.astype(BF16), preferred_element_type=F32)
        out_ref[level, 0, :, lanes_of(chunk)] = result
        if chunk == CHUNKS - 1:
            store(level).start()
        publish(2 * (levels - 1) - level, chunk, result)

    for ref, index in order:
        fetch(ref, index).start()
    sums[slots] = jnp.zeros((width, lanes), F32)
    for chunk in range(CHUNKS):
        solve_lower(0, chunk, load(0, 0)[0, :, lanes_of(chunk)].astype(F32))
    pl.semaphore_wait(barrier, len(peers))

    def turn(step, chunk, other_step):
        other = 1 - chunk

        moving = other_step < rounds
        gather_finish(step, chunk)
        update_near(step, chunk)
        if moving:
            cross(other_step, other)
            relay(other_step, other, 1)
        update_far(step, chunk)
        if moving:
            for hops in range(2, longest):
                relay(other_step, other, hops)
        finish_sum(step, chunk)
        if step + 1 < rounds:
            gather_minor(step + 1, chunk)
            gather_major(step + 1, chunk)

    for chunk in range(CHUNKS):
        gather_minor(0, chunk)
        gather_major(0, chunk)
    cross(0, 0)
    for hops in range(1, longest):
        relay(0, 0, hops)
    for step in range(rounds):
        turn(step, 0, step)
        turn(step, 1, step + 1)
    for kind in ("gather", "sum"):
        for chunk in range(CHUNKS):
            drain(kind, rounds - 1, chunk)
    for level in range(levels):
        store(level).wait()


def shards(*args):
    rows, cols = lax.axis_size("row"), lax.axis_size("col")
    levels, per_device, width, rhs_cols = args[0].shape
    slots = args[1].shape[3]
    assert per_device == 1 and rows % 4 == 0 and rhs_cols % CHUNKS == 0 and levels > 2
    lanes = rhs_cols // CHUNKS
    rounds = 2 * (levels - 1)
    major = 4 if rows % 4 == 0 else 1
    minor = rows // major
    copies = 1 + 2 * minor + 2 * (major - 1) * minor
    smem = pl.BlockSpec(memory_space=pltpu.SMEM)
    anywhere = pl.BlockSpec(memory_space=pl.ANY)
    args = [arg.reshape(levels - 1, 1, slots) if arg.dtype == jnp.int32 else arg for arg in args]
    scratch = [pltpu.VMEM((rows, width, lanes), BF16) for _ in range(rounds * CHUNKS)]
    scratch += [
        pltpu.VMEM((levels, CHUNKS, width, lanes), F32),
        pltpu.VMEM((levels - 2, cols, CHUNKS, width, lanes), F32),
        pltpu.VMEM((slots + 1, width, lanes), F32),
        pltpu.VMEM((CHUNKS, width, lanes), BF16),
        pltpu.VMEM((rounds, CHUNKS, cols - 1, width, lanes), BF16),
        pltpu.VMEM((rounds, CHUNKS, cols - 1, width, lanes), BF16),
        pltpu.SemaphoreType.DMA((CHUNKS, copies)),
        pltpu.SemaphoreType.DMA((rounds, CHUNKS, rows)),
        pltpu.SemaphoreType.DMA((CHUNKS, cols - 1)),
        pltpu.SemaphoreType.DMA((rounds, CHUNKS, cols - 1)),
    ]
    scratch += [pltpu.VMEM(args[i].shape[-4:], BF16) for i in (0, 4)]
    scratch += [pltpu.VMEM(args[1].shape[-4:], BF16)]
    scratch += [pltpu.VMEM(args[8].shape, BF16), pltpu.VMEM(args[5].shape[-4:], BF16)]
    scratch += [
        pltpu.VMEM(args[0].shape, F32),
        pltpu.SemaphoreType.DMA((5, levels)),
        pltpu.SemaphoreType.DMA((levels,)),
    ]
    return pl.pallas_call(
        functools.partial(kernel, rows, cols, levels, slots, width, lanes),
        out_shape=jax.ShapeDtypeStruct(args[0].shape, F32),
        in_specs=[anywhere, anywhere, smem, smem, anywhere, anywhere, smem, smem, anywhere],
        out_specs=anywhere,
        scratch_shapes=scratch,
        compiler_params=pltpu.CompilerParams(
            collective_id=0, has_side_effects=True, vmem_limit_bytes=60 * 1024 * 1024
        ),
    )(*args)


def solution(mesh):
    in_specs = (
        P(None, ("row", "col"), None, None),
        P("row", "col", None, None, None, None),
        P("row", "col", None, None),
        P("row", "col", None, None),
        P(None, ("row", "col"), None, None),
        P("row", "col", None, None, None, None),
        P("row", "col", None, None),
        P("row", "col", None, None),
        P(None, ("row", "col"), None, None),
    )
    out_specs = P(None, ("row", "col"), None, None)
    return jax.shard_map(shards, mesh=mesh, in_specs=in_specs, out_specs=out_specs, check_vma=False)
```

```python
import functools

import jax
import jax.numpy as jnp
from jax import lax
from jax.experimental import pallas as pl
from jax.experimental.pallas import tpu as pltpu
from jax.sharding import PartitionSpec as P

MESH = pl.DeviceIdType.MESH
CHUNKS = 2
F32 = jnp.float32
BF16 = jnp.bfloat16


def kernel(
    rows,
    cols,
    levels,
    slots,
    width,
    lanes,
    rhs_hbm,
    lower_hbm,
    lower_source,
    lower_target,
    diag_lower_hbm,
    upper_hbm,
    upper_source,
    upper_target,
    diag_upper_hbm,
    out_hbm,
    *scratch,
):
    rounds = 2 * (levels - 1)
    panels = scratch[: rounds * CHUNKS]
    rest = scratch[rounds * CHUNKS :]
    forward, far, sums, owned, outbox, inbox, gather_send, gather_recv, sum_send, sum_recv = rest[:10]
    inputs, out_ref, load_sem, store_sem = rest[10:15], rest[15], rest[16], rest[17]
    sources = (rhs_hbm, diag_lower_hbm, lower_hbm.at[0, 0], diag_upper_hbm, upper_hbm.at[0, 0])
    order = [(0, 0), (1, 0), (2, 0)]
    for level in range(1, levels):
        order += [(0, level), (1, level)] + ([(2, level)] if level < levels - 1 else [])
    for level in range(levels - 1, -1, -1):
        order += [(3, level)] + ([(4, level - 1)] if level else [])
    loaded = set()

    def fetch(ref, index):
        return pltpu.make_async_copy(sources[ref].at[index], inputs[ref].at[index], load_sem.at[ref, index])

    def load(ref, index):
        if (ref, index) not in loaded:
            loaded.add((ref, index))
            fetch(ref, index).wait()
        return inputs[ref].at[index]

    def store(level):
        return pltpu.make_async_copy(out_ref.at[level], out_hbm.at[level], store_sem.at[level])

    major = 4 if rows % 4 == 0 else 1
    minor = rows // major
    row, col = lax.axis_index("row"), lax.axis_index("col")
    row_major, row_minor = row // minor, row % minor

    def row_at(major_step, minor_step):
        return ((row_major + major_step) % major) * minor + (row_minor + minor_step) % minor

    peers = [(row_at(step, 0), col) for step in range(1, major)]
    peers += [(row_at(0, step), col) for step in range(1, minor)]
    peers += [(row, (col + step) % cols) for step in range(1, cols)]
    barrier = pltpu.get_barrier_semaphore()
    for peer in peers:
        pl.semaphore_signal(barrier, inc=1, device_id=peer, device_id_type=MESH)

    def lanes_of(chunk):
        return slice(chunk * lanes, (chunk + 1) * lanes)

    def plan(step):
        if step < levels - 1:
            return step, step + 1, 2, lower_source, lower_target, step == 0, list(range(step + 2, levels))
        source = 2 * (levels - 1) - step
        first = step == levels - 1
        return source - 1, source - 1, 4, upper_source, upper_target, first, list(range(source - 1))

    def far_slot(step, level):
        return level - 2 if step < levels - 1 else level

    pending = {}

    def push(step, chunk, slot, target, index, needed=None):
        ref = panels[step * CHUNKS + chunk]

        def make():
            return pltpu.make_async_remote_copy(
                src_ref=ref.at[slot],
                dst_ref=ref.at[slot],
                send_sem=gather_send.at[chunk, index],
                recv_sem=gather_recv.at[step, chunk, slot],
                device_id=(target, col),
                device_id_type=MESH,
            )

        pending.setdefault(("gather", step, chunk), []).append((make, needed))
        when(needed, lambda: make().start())

    def when(needed, action):
        if needed is None:
            action()
        else:
            pl.when(needed)(action)

    def arrived(step, chunk, slot):
        ref = panels[step * CHUNKS + chunk]
        pltpu.make_async_remote_copy(
            src_ref=ref.at[slot],
            dst_ref=ref.at[slot],
            send_sem=gather_send.at[chunk, 0],
            recv_sem=gather_recv.at[step, chunk, slot],
            device_id=(row, col),
            device_id_type=MESH,
        ).wait_recv()

    def drain(kind, step, chunk):
        for make, needed in pending.pop((kind, step, chunk), []):
            when(needed, lambda: make().wait_send())

    longest = major - 1
    at_end = (row_major == 0) | (row_major == longest)
    opposite = (longest - row_major) * minor + row_minor
    forwarded = 2 + minor

    def gather_major(step, chunk):
        push(step, chunk, row, row + minor, 0, row_major < longest)
        push(step, chunk, row, row - minor, 1, row_major > 0)
        if longest > 1:
            push(step, chunk, row, opposite, 2, at_end)

    def gather_minor(step, chunk):
        for across in range(1, minor):
            push(step, chunk, row, row_at(0, across), 1 + across)

    def cross(step, chunk):
        for across in range(1, minor):
            slot = row_at(0, across)
            arrived(step, chunk, slot)
            if longest > 1:
                push(step, chunk, slot, opposite, forwarded + across - 1, at_end)

    def relay(step, chunk, hops):
        for side, sign in enumerate((-1, 1)):
            origin = row_major + sign * hops
            slot = row + sign * hops * minor
            came = (origin >= 0) & (origin < major)
            base = forwarded + minor - 1 + ((hops - 1) * 2 + side) * minor
            when(came, lambda: arrived(step, chunk, slot))
            if hops + 1 < max(longest, 2):
                after = row_major - sign
                push(step, chunk, slot, row - sign * minor, base, came & (after >= 0) & (after < major))
            for across in range(1, minor):
                push(step, chunk, slot, row_at(0, across), base + across, came)

    def gather_finish(step, chunk):
        if longest > 1:
            when(at_end, lambda: arrived(step, chunk, opposite))
        for across in range(1, minor):
            for offset in range(1, major):
                arrived(step, chunk, row_at(offset, across))

    def last_slot(target, at, wanted, before):
        found = jnp.int32(slots)
        for k in range(before):
            found = jnp.where(target[at, 0, k] == wanted, k, found)
        return found

    def update_near(step, chunk):
        at, level, blocks, source, target, first, _ = plan(step)
        ref = panels[step * CHUNKS + chunk]
        held = load(blocks, at)
        for k in range(slots):
            total = jnp.dot(held[k], ref[source[at, 0, k]], preferred_element_type=F32)
            if k > 0:
                total = total + sums[last_slot(target, at, target[at, 0, k], k)]
            sums[k] = total
        drain("sum", step - 1, chunk)
        for offset in list(range(1, cols)) + [0]:
            owner = (col + offset) % cols
            total = sums[last_slot(target, at, level * cols + owner, slots)]
            if not first:
                total = total + far[far_slot(step, level), owner, chunk]
            if offset == 0:
                owned[chunk] = total.astype(BF16)
                continue
            outbox[step, chunk, offset - 1] = total.astype(BF16)
            copy = pltpu.make_async_remote_copy(
                src_ref=outbox.at[step, chunk, offset - 1],
                dst_ref=inbox.at[step, chunk, offset - 1],
                send_sem=sum_send.at[chunk, offset - 1],
                recv_sem=sum_recv.at[step, chunk, offset - 1],
                device_id=(row, owner),
                device_id_type=MESH,
            )
            copy.start()
            pending.setdefault(("sum", step, chunk), []).append((lambda copy=copy: copy, None))

    def update_far(step, chunk):
        at, _, _, _, target, first, others = plan(step)
        for level in others:
            place = far_slot(step, level)

            @pl.loop(0, cols)
            def _(q):
                total = sums[last_slot(target, at, level * cols + q, slots)]
                if not first:
                    total = total + far[place, q, chunk]
                far[place, q, chunk] = total

    def finish_sum(step, chunk):
        level = plan(step)[1]
        total = owned[chunk].astype(F32)
        for make, _ in pending[("sum", step, chunk)]:
            make().wait_recv()
        for offset in range(1, cols):
            total = total + inbox[step, chunk, offset - 1].astype(F32)
        if step < levels - 1:
            solve_lower(level, chunk, load(0, level)[0, :, lanes_of(chunk)].astype(F32) - total)
        else:
            solve_upper(level, chunk, forward[level, chunk] - total)

    def publish(step, chunk, result):
        if step < rounds:
            panels[step * CHUNKS + chunk][row] = result.astype(BF16)
            drain("gather", step - 1, chunk)

    def solve_lower(level, chunk, lowered):
        result = jnp.dot(load(1, level)[0], lowered.astype(BF16), preferred_element_type=F32)
        forward[level, chunk] = result
        if level == levels - 1:
            solve_upper(level, chunk, result)
        else:
            publish(level, chunk, result)

    def solve_upper(level, chunk, raised):
        result = jnp.dot(load(3, level)[0], raised.astype(BF16), preferred_element_type=F32)
        out_ref[level, 0, :, lanes_of(chunk)] = result
        if chunk == CHUNKS - 1:
            store(level).start()
        publish(2 * (levels - 1) - level, chunk, result)

    for ref, index in order:
        fetch(ref, index).start()
    sums[slots] = jnp.zeros((width, lanes), F32)
    for chunk in range(CHUNKS):
        solve_lower(0, chunk, load(0, 0)[0, :, lanes_of(chunk)].astype(F32))
    pl.semaphore_wait(barrier, len(peers))

    def turn(step, chunk, other_step):
        other = 1 - chunk

        moving = other_step < rounds
        gather_finish(step, chunk)
        update_near(step, chunk)
        if moving:
            cross(other_step, other)
            relay(other_step, other, 1)
        update_far(step, chunk)
        finish_sum(step, chunk)
        if step + 1 < rounds:
            gather_minor(step + 1, chunk)
            gather_major(step + 1, chunk)
        if moving:
            for hops in range(2, longest):
                relay(other_step, other, hops)

    for chunk in range(CHUNKS):
        gather_minor(0, chunk)
        gather_major(0, chunk)
    cross(0, 0)
    for hops in range(1, longest):
        relay(0, 0, hops)
    for step in range(rounds):
        turn(step, 0, step)
        turn(step, 1, step + 1)
    for kind in ("gather", "sum"):
        for chunk in range(CHUNKS):
            drain(kind, rounds - 1, chunk)
    for level in range(levels):
        store(level).wait()


def shards(*args):
    rows, cols = lax.axis_size("row"), lax.axis_size("col")
    levels, per_device, width, rhs_cols = args[0].shape
    slots = args[1].shape[3]
    assert per_device == 1 and rows % 4 == 0 and rhs_cols % CHUNKS == 0 and levels > 2
    lanes = rhs_cols // CHUNKS
    rounds = 2 * (levels - 1)
    major = 4 if rows % 4 == 0 else 1
    minor = rows // major
    copies = 1 + 2 * minor + 2 * (major - 1) * minor
    smem = pl.BlockSpec(memory_space=pltpu.SMEM)
    anywhere = pl.BlockSpec(memory_space=pl.ANY)
    args = [arg.reshape(levels - 1, 1, slots) if arg.dtype == jnp.int32 else arg for arg in args]
    scratch = [pltpu.VMEM((rows, width, lanes), BF16) for _ in range(rounds * CHUNKS)]
    scratch += [
        pltpu.VMEM((levels, CHUNKS, width, lanes), F32),
        pltpu.VMEM((levels - 2, cols, CHUNKS, width, lanes), F32),
        pltpu.VMEM((slots + 1, width, lanes), F32),
        pltpu.VMEM((CHUNKS, width, lanes), BF16),
        pltpu.VMEM((rounds, CHUNKS, cols - 1, width, lanes), BF16),
        pltpu.VMEM((rounds, CHUNKS, cols - 1, width, lanes), BF16),
        pltpu.SemaphoreType.DMA((CHUNKS, copies)),
        pltpu.SemaphoreType.DMA((rounds, CHUNKS, rows)),
        pltpu.SemaphoreType.DMA((CHUNKS, cols - 1)),
        pltpu.SemaphoreType.DMA((rounds, CHUNKS, cols - 1)),
    ]
    scratch += [pltpu.VMEM(args[i].shape[-4:], BF16) for i in (0, 4)]
    scratch += [pltpu.VMEM(args[1].shape[-4:], BF16)]
    scratch += [pltpu.VMEM(args[8].shape, BF16), pltpu.VMEM(args[5].shape[-4:], BF16)]
    scratch += [
        pltpu.VMEM(args[0].shape, F32),
        pltpu.SemaphoreType.DMA((5, levels)),
        pltpu.SemaphoreType.DMA((levels,)),
    ]
    return pl.pallas_call(
        functools.partial(kernel, rows, cols, levels, slots, width, lanes),
        out_shape=jax.ShapeDtypeStruct(args[0].shape, F32),
        in_specs=[anywhere, anywhere, smem, smem, anywhere, anywhere, smem, smem, anywhere],
        out_specs=anywhere,
        scratch_shapes=scratch,
        compiler_params=pltpu.CompilerParams(
            collective_id=0, has_side_effects=True, vmem_limit_bytes=60 * 1024 * 1024
        ),
    )(*args)


def solution(mesh):
    in_specs = (
        P(None, ("row", "col"), None, None),
        P("row", "col", None, None, None, None),
        P("row", "col", None, None),
        P("row", "col", None, None),
        P(None, ("row", "col"), None, None),
        P("row", "col", None, None, None, None),
        P("row", "col", None, None),
        P("row", "col", None, None),
        P(None, ("row", "col"), None, None),
    )
    out_specs = P(None, ("row", "col"), None, None)
    return jax.shard_map(shards, mesh=mesh, in_specs=in_specs, out_specs=out_specs, check_vma=False)
```
